32 devices in a mesh: ctx: 8 (over z, x), head: 4 (over y, core).
Axes of the slice: x: 2, y: 2, z: 4, core: 2. Of those that a mesh axis runs over, the one named last changes fastest.
Arguments:
- x_raw: bfloat16 [2048, 4096], P('ctx', 'head'), may hold values from -30 to 30
- bc_raw: bfloat16 [2048, 256], P('ctx'), may hold values from -6 to 6
- gate_raw: bfloat16 [2048, 4096], P('ctx', 'head'), may hold values from -16 to 16
- log_decay: float32 [64, 2048], P('head', 'ctx'), may hold values from -0.8 to 0
- level_weights: float32 [16, 64, 2048], P(None, 'head', 'ctx'), may hold values from 0.25 to 2
- conv_x: float32 [4, 4096], P(None, 'head'), may hold values from -3 to 3
- conv_bc: float32 [4, 256], replicated, may hold values from -3 to 3
- norm_gain: float32 [4096], P('head'), may hold values from 0.5 to 1.5
- out_grad: bfloat16 [2048, 4096], P('ctx', 'head'), may hold values from -6 to 6
Outputs:
- layer_out: bfloat16 [2048, 4096], P('ctx', 'head')
- x_grad: bfloat16 [2048, 4096], P('ctx', 'head')
- bc_grad: bfloat16 [2048, 256], P('ctx')
The draws below stay inside these ranges and needn't reach their ends.
All inputs are finite; a program needn't handle non-finite values.
Results may differ from the reference program's by a relative error of at most 0.0013.
Values may be sent and summed in bfloat16 or wider, within the bound.
No kernel may reach another device: no remote copies, remote signals or barrier semaphores. Data moves between devices by JAX's collectives and lax.ppermute only.
A program may use at most 128 MiB of HBM per device.

```python
import math
import jax
import jax.numpy as jnp
from jax import lax

HEADS = 64
HEAD_DIM = 64
STATE = 128
KERNEL = 4
NLEV = 16
TOK_DEV = 256
SEQ = 2048
INNER = 4096
N_CTX = 8


def draw_x_raw(key, part):
    keys = jax.random.split(key, 3)
    width = HEADS * HEAD_DIM
    noise = jax.random.normal(keys[0], (SEQ, width), jnp.float32)
    trend = jnp.arange(width, dtype=jnp.float32) / width
    column_factor = 10.0 ** (0.5 * trend + 0.5 * jax.random.uniform(keys[1], (width,), jnp.float32) - 0.52)
    row_scale = 10.0 ** (jax.random.uniform(keys[2], (SEQ, 1), jnp.float32) - 0.5)
    return jnp.clip(noise * column_factor * row_scale, -30.0, 30.0).astype(jnp.bfloat16)


def draw_gate_raw(key, part):
    keys = jax.random.split(key, 2)
    width = HEADS * HEAD_DIM
    row_scale = 10.0 ** (jax.random.uniform(keys[1], (SEQ, 1), jnp.float32) - 0.5)
    starting_amount = jax.random.normal(keys[0], (SEQ, width), jnp.float32)
    return jnp.clip(starting_amount * row_scale, -16.0, 16.0).astype(jnp.bfloat16)


def draw_log_decay(key, part):
    keys = jax.random.split(key, 8)
    order = jax.random.permutation(keys[0], HEADS)
    slow_count = HEADS // 2
    is_slow = order < slow_count
    slow_rate = jnp.exp(jax.random.uniform(keys[1], (HEADS,), jnp.float32, jnp.log(0.05 / SEQ), jnp.log(0.3 / SEQ)))
    fast_rate = jnp.exp(jax.random.uniform(keys[2], (HEADS,), jnp.float32, jnp.log(1.0 / TOK_DEV), jnp.log(1.0 / 30.0)))
    rates = jnp.where(is_slow, slow_rate, fast_rate)
    blocks = SEQ // TOK_DEV
    processor_factor = jnp.exp(jax.random.uniform(keys[3], (HEADS, blocks, 1), jnp.float32, jnp.log(0.5), jnp.log(2.0)))
    token_factor = jax.random.uniform(keys[4], (HEADS, blocks, TOK_DEV), jnp.float32, 0.5, 1.5)
    starting_amount = -(rates[:, None, None] * processor_factor * token_factor).reshape(HEADS, SEQ)
    initial_spot = jax.random.randint(keys[5], (), 0, SEQ // 2)
    latter_spot = jax.random.randint(keys[6], (), SEQ // 2, SEQ)
    objective_readings = jax.random.uniform(keys[7], (2,), jnp.float32, 0.2, 0.5)
    spot_sequence = jnp.arange(SEQ, dtype=jnp.int32)
    packet_batches = jnp.where(spot_sequence == initial_spot, jnp.log(1.0 - objective_readings[0]), 0.0)
    packet_batches = packet_batches + jnp.where(spot_sequence == latter_spot, jnp.log(1.0 - objective_readings[1]), 0.0)
    return starting_amount + packet_batches[None, :]


def shard_levels(stream_key, extent, shards, smallest, top_value):
    loudness, own = 1.0, jax.random.fold_in(stream_key, 6)
    for axis_at, parts in shards:
        draws = jnp.exp(jax.random.uniform(jax.random.fold_in(own, axis_at), (parts,), jnp.float32, smallest / len(shards), top_value / len(shards)))
        loudness = loudness * jnp.repeat(draws, extent[axis_at] // parts).reshape([-1 if axis == axis_at else 1 for axis in range(len(extent))])
    return loudness


def bell_draw(rng, extent, deviation, bound, cuts=(), held_as=jnp.bfloat16):
    entries = deviation * jax.random.normal(rng, extent, jnp.float32)
    if cuts:
        entries = entries * shard_levels(rng, extent, cuts, -0.22, 0.18)
    return jnp.clip(entries, -bound, bound).astype(held_as)


def setup_inputs(seed: int = 0) -> dict:
    splits = jax.random.split(jax.random.key(seed), 10)
    x_raw = draw_x_raw(jax.random.fold_in(splits[9], 71), 0)
    bc_raw = bell_draw(splits[1], (SEQ, 2 * STATE), 1.0, 6.0, ((0, 8),))
    gate_raw = draw_gate_raw(jax.random.fold_in(splits[9], 71), 0)
    log_decay = draw_log_decay(jax.random.fold_in(splits[9], 71), 0)
    level_weights = jnp.clip(jnp.exp(math.log(2.0) - 2.0794415 * jax.random.uniform(splits[4], (NLEV, HEADS, SEQ), jnp.float32) ** shard_levels(splits[4], (NLEV, HEADS, SEQ), ((1, 4), (2, 8)), -0.2, 0.2)), 0.25, 2.0)
    conv_x = bell_draw(splits[5], (KERNEL, INNER), KERNEL ** -0.5, 3.0, ((1, 4),), jnp.float32)
    conv_bc = bell_draw(splits[6], (KERNEL, 2 * STATE), KERNEL ** -0.5, 3.0, (), jnp.float32)
    norm_gain = jnp.clip(1.0 + 0.1 * jax.random.normal(splits[7], (INNER,), jnp.float32), 0.5, 1.5)
    out_grad = bell_draw(splits[8], (SEQ, INNER), 1.0, 6.0, ((0, 8), (1, 4)))
    return dict(x_raw=x_raw, bc_raw=bc_raw, gate_raw=gate_raw, log_decay=log_decay, level_weights=level_weights, conv_x=conv_x, conv_bc=conv_bc, norm_gain=norm_gain, out_grad=out_grad)


highest = lax.Precision.HIGHEST
epsilon = 1e-05

def bit_length(values, count):
    summed = jnp.zeros(values.shape, jnp.int32)
    for bit_pos in range(count):
        summed = summed + (values >= 2 ** bit_pos).astype(jnp.int32)
    return summed

def conv_pre(raw_rows, weights):
    tap_count = weights.shape[0]
    length = raw_rows.shape[0]
    padded = jnp.concatenate([jnp.zeros((tap_count - 1, raw_rows.shape[1]), raw_rows.dtype), raw_rows], axis=0)
    summed = jnp.zeros(raw_rows.shape, raw_rows.dtype)
    for tap_id in range(tap_count):
        summed = summed + weights[tap_id] * padded[tap_id:tap_id + length]
    return summed

def state_mixer(x_conv, b_state, c_state, log_decay, level_weights):
    width = TOK_DEV
    low_bits = width.bit_length() - 1
    ctx_bits = N_CTX.bit_length() - 1
    blocks = SEQ // width
    float_type = x_conv.dtype
    position = jnp.arange(width, dtype=jnp.int32)
    inside = bit_length(jnp.bitwise_xor(position[:, None], position[None, :]), low_bits)
    inside_all = jnp.broadcast_to(inside[None], (HEADS, width, width))
    causal = (position[:, None] >= position[None, :])[None]
    far_ids = [min(low_bits + 1 + bit_pos, NLEV - 1) for bit_pos in range(ctx_bits)]
    level_ids = jnp.arange(ctx_bits, dtype=jnp.int32)

    def block_fn(stack, inputs):
        x_block, b_block, c_block, decay_block, weight_block, block_id = inputs
        cum_decay = jnp.cumsum(decay_block, axis=1)
        block_total = cum_decay[:, -1]
        scores = jnp.dot(c_block, b_block.T, precision=highest, preferred_element_type=jnp.float32)
        near = jnp.transpose(weight_block[:low_bits + 1], (1, 2, 0))
        chosen = jnp.take_along_axis(near, inside_all, axis=2)
        exponent = jnp.where(causal, cum_decay[:, :, None] - cum_decay[:, None, :], -jnp.inf)
        mixing = chosen * jnp.exp(exponent) * scores[None]
        x_heads = x_block.reshape(width, HEADS, HEAD_DIM)
        intra = jnp.einsum('hts,shp->thp', mixing, x_heads, precision=highest).reshape(width, INNER)
        bit_flags = jnp.stack([block_id // 2 ** bit_pos % 2 for bit_pos in range(ctx_bits)]).astype(float_type)
        far_weights = jnp.stack([weight_block[far_id] for far_id in far_ids])
        far_coef = far_weights * jnp.exp(cum_decay)[None] * bit_flags[:, None, None]
        projected = jnp.einsum('tn,knm->ktm', c_block, stack, precision=highest)
        coef_wide = jnp.repeat(far_coef, HEAD_DIM, axis=1)
        inter = jnp.einsum('ktm,kmt->tm', projected, coef_wide, precision=highest)
        end_weight = jnp.repeat(jnp.exp(block_total[:, None] - cum_decay), HEAD_DIM, axis=0).T
        end_state = jnp.dot(b_block.T, x_block * end_weight, precision=highest, preferred_element_type=jnp.float32)
        run_flag = jnp.ones((), jnp.int32)
        trailing = jnp.zeros((), jnp.int32)
        for bit_pos in range(ctx_bits):
            run_flag = run_flag * (block_id // 2 ** bit_pos % 2)
            trailing = trailing + run_flag
        retain_multiplier = jnp.repeat(jnp.exp(block_total), HEAD_DIM)
        cleared = (level_ids < trailing)[:, None, None]
        lower_sum = lax.optimization_barrier(jnp.sum(jnp.where(cleared, stack, 0.0), axis=0))
        new_block = lower_sum * retain_multiplier + end_state
        stack = jnp.where(cleared, 0.0, stack * retain_multiplier)
        stack = jnp.where((level_ids == trailing)[:, None, None], new_block[None], stack)
        return (stack, intra + inter)
    inputs = (x_conv.reshape(blocks, width, INNER), b_state.reshape(blocks, width, STATE), c_state.reshape(blocks, width, STATE), jnp.transpose(log_decay.reshape(HEADS, blocks, width), (1, 0, 2)), jnp.transpose(level_weights.reshape(NLEV, HEADS, blocks, width), (2, 0, 1, 3)), jnp.arange(blocks, dtype=jnp.int32))
    empty_stack = jnp.zeros((ctx_bits, STATE, INNER), float_type)
    final_stack, outputs = lax.scan(jax.checkpoint(block_fn), empty_stack, inputs)
    return outputs.reshape(SEQ, INNER)

def layer(x_raw, bc_raw, gate_act, log_decay, level_weights, conv_x, conv_bc, norm_gain):
    x_conv = jax.nn.silu(conv_pre(x_raw, conv_x))
    bc_conv = jax.nn.silu(conv_pre(bc_raw, conv_bc))
    ssd_out = state_mixer(x_conv, bc_conv[:, :STATE], bc_conv[:, STATE:], log_decay, level_weights)
    mixed = ssd_out * gate_act
    mean_square = lax.optimization_barrier(jnp.mean(mixed * mixed, axis=1, keepdims=True))
    return norm_gain * mixed * lax.rsqrt(mean_square + epsilon)

def reference(x_raw, bc_raw, gate_raw, log_decay, level_weights, conv_x, conv_bc, norm_gain, out_grad):
    gate_act = jax.nn.silu(gate_raw.astype(jnp.float32))

    def forward(values_in, states_in):
        return layer(values_in, states_in, gate_act, log_decay, level_weights, conv_x, conv_bc, norm_gain)
    result, pullback = jax.vjp(forward, x_raw.astype(jnp.float32), bc_raw.astype(jnp.float32))
    x_grad, bc_grad = pullback(out_grad.astype(jnp.float32))
    return (result.astype(jnp.bfloat16), x_grad.astype(jnp.bfloat16), bc_grad.astype(jnp.bfloat16))
```

```python
import functools

import jax
import jax.numpy as jnp
from jax import lax
from jax.experimental import pallas as pl
from jax.experimental.pallas import tpu as pltpu
from jax.sharding import PartitionSpec as P

HEADS = 64
HEAD_DIM = 64
STATE = 128
EPSILON = 1e-05
RIM = 16
F32 = jnp.float32
BF16 = jnp.bfloat16
HIGH = lax.Precision.HIGH
HIGHEST = lax.Precision.HIGHEST


def dot(a, b, contract=(1, 0), precision=HIGH):
    return lax.dot_general(
        a,
        b,
        (((contract[0],), (contract[1],)), ((), ())),
        precision=precision,
        preferred_element_type=F32,
    )


def split(value):
    high = value.astype(BF16)
    return high, (value - high.astype(F32)).astype(BF16)


def dot_exact(a, b, contract=(1, 0)):
    return lax.dot_general(
        a, b, (((contract[0],), (contract[1],)), ((), ())), preferred_element_type=F32
    )


def eye(size):
    row = lax.broadcasted_iota(jnp.int32, (size, size), 0)
    col = lax.broadcasted_iota(jnp.int32, (size, size), 1)
    return (row == col).astype(F32).astype(BF16)


def turn(value, identity):
    high, low = split(value)
    width = identity.shape[0]
    parts = []
    for at in range(0, value.shape[1], width):
        piece = slice(at, at + width)
        parts.append(
            dot_exact(identity, high[:, piece], (1, 1)) + dot_exact(identity, low[:, piece], (1, 1))
        )
    return parts[0] if len(parts) == 1 else jnp.concatenate(parts, axis=0)


def turn_exact(value, identity):
    width = identity.shape[0]
    parts = [
        dot_exact(identity, value[:, at : at + width], (1, 1))
        for at in range(0, value.shape[1], width)
    ]
    return parts[0] if len(parts) == 1 else jnp.concatenate(parts, axis=0)


def sigmoid(value):
    return 1.0 / (1.0 + jnp.exp(-value))


def by_head(rows, values):
    heads, width = rows.shape
    shaped = values.reshape(heads, values.shape[0] // heads, width)
    return (shaped * rows[:, None, :]).reshape(values.shape)


def call(body, outs, ins, scratch=(), flops=0):
    moved = sum(o.size * o.dtype.itemsize for o in (*outs, *ins))
    return pl.pallas_call(
        body,
        out_shape=[jax.ShapeDtypeStruct(o.shape, o.dtype) for o in outs],
        in_specs=[pl.BlockSpec(memory_space=pltpu.VMEM)] * len(ins),
        out_specs=[pl.BlockSpec(memory_space=pltpu.VMEM)] * len(outs),
        scratch_shapes=list(scratch),
        compiler_params=pltpu.CompilerParams(vmem_limit_bytes=40 * 2**20),
        cost_estimate=pl.CostEstimate(flops=flops, bytes_accessed=moved, transcendentals=0),
    )(*ins)


def shape(*dims, dtype=F32):
    return jax.ShapeDtypeStruct(dims, dtype)


def pre_kernel(
    x_ref, rim_ref, bc_ref, decay_ref, taps_x_ref, taps_bc_ref,
    xt_ref, slope_ref, bc_conv_ref, bct_ref, bc_slope_ref, cum_ref, sent_ref,
    xs_ref, bcs_ref,
):
    length, columns = x_ref.shape
    heads = decay_ref.shape[0]
    taps = taps_x_ref.shape[0]
    state = STATE
    first = RIM - taps + 1
    row = lax.broadcasted_iota(jnp.int32, (length, length), 0)
    col = lax.broadcasted_iota(jnp.int32, (length, length), 1)
    cum = dot(decay_ref[...], (row <= col).astype(F32), precision=HIGHEST)
    cum_ref[...] = cum
    total = cum[:, length - 1 :]
    end_weight = jnp.exp(total - cum)

    bcs_ref[:RIM] = rim_ref[:, columns:].astype(F32)
    bcs_ref[RIM:] = bc_ref[...].astype(F32)
    pre = sum(taps_bc_ref[k : k + 1] * bcs_ref[first + k : first + k + length] for k in range(taps))
    gate = sigmoid(pre)
    conv = pre * gate
    bc_conv_ref[...] = conv
    bc_slope_ref[...] = gate * (1.0 + pre * (1.0 - gate))
    identity = eye(128)
    bct_ref[...] = turn(conv, identity)
    b_high, b_low = split(conv[:, :state])
    b_both = jnp.concatenate([b_high, b_low], axis=1)

    xs_ref[:RIM] = rim_ref[:, :columns].astype(F32)
    xs_ref[RIM:] = x_ref[...].astype(F32)
    step = 128
    for at in range(0, columns, step):
        part = slice(at, at + step)
        pre = sum(
            taps_x_ref[k : k + 1, part] * xs_ref[first + k : first + k + length, part]
            for k in range(taps)
        )
        gate = sigmoid(pre)
        conv = pre * gate
        slope_ref[:, part] = gate * (1.0 + pre * (1.0 - gate))
        turned = turn(conv, identity)
        xt_ref[part] = turned
        at_head = at // HEAD_DIM
        weighted = by_head(end_weight[at_head : at_head + step // HEAD_DIM], turned)
        high, low = split(weighted)
        both = dot_exact(high, b_both)
        sent_ref[part] = both[:, :state] + both[:, state:] + dot_exact(low, b_high)
    sent_ref[columns:] = jnp.broadcast_to(total, (heads, state))


def over_heads(scales, values):
    return by_head(scales, values)


def upper_half(bit):
    return (lax.axis_index("ctx") // 2**bit) % 2 == 1


def join_kernel(bit, own_ref, other_ref, joined_ref):
    heads = own_ref.shape[0] // (HEAD_DIM + 1)
    columns = heads * HEAD_DIM
    upper = upper_half(bit)
    own_total, other_total = own_ref[columns:], other_ref[columns:]
    for_other = jnp.where(upper, jnp.exp(own_total), 1.0)
    for_own = jnp.where(upper, 1.0, jnp.exp(other_total))
    joined_ref[:columns] = over_heads(for_other, other_ref[:columns]) + over_heads(
        for_own, own_ref[:columns]
    )
    joined_ref[columns:] = own_total + other_total


def head_weights(head, cum_ref, cum_t, levels_ref, distance, causal):
    length = cum_ref.shape[1]
    half = length // 2
    low_bits = length.bit_length() - 1
    row = cum_ref[pl.ds(head, 1), :]
    lanes = lax.broadcasted_iota(jnp.int32, cum_t.shape, 1)
    col = jnp.sum(jnp.where(lanes == head, cum_t, 0.0), axis=1, keepdims=True)
    weights = [levels_ref[level, pl.ds(head, 1), :] for level in range(low_bits + 1)]
    blocks = []
    for at in (0, half):
        part = slice(at, at + half)
        chosen = jnp.broadcast_to(weights[0][:, part], (half, half))
        for level in range(1, low_bits):
            chosen = jnp.where(distance >= 2 ** (level - 1), weights[level][:, part], chosen)
        gap = jnp.where(causal, row[:, part] - col[part], -jnp.inf)
        blocks.append(chosen * jnp.exp(gap))
    late = slice(half, length)
    far = weights[low_bits][:, late] * jnp.exp(row[:, late] - col[:half])
    return blocks[0], far, blocks[1]


def block_masks(half):
    row = lax.broadcasted_iota(jnp.int32, (half, half), 0)
    col = lax.broadcasted_iota(jnp.int32, (half, half), 1)
    return jnp.bitwise_xor(row, col), col >= row


def scores_of(bct, state):
    return dot(bct[:state], bct[state:], (0, 0))


def intra_kernel(
    first_head, xt_ref, bct_ref, cum_ref, levels_ref, out_ref, scores_ref, cum_t_ref
):
    heads = out_ref.shape[0] // HEAD_DIM
    length = cum_ref.shape[1]
    half = length // 2
    scores_ref[...] = scores_of(bct_ref[...], STATE)
    cum_t_ref[...] = jnp.transpose(cum_ref[...])
    distance, causal = block_masks(half)

    def one(at, carry):
        head = first_head + at
        low, far, high = head_weights(
            head, cum_ref, cum_t_ref[...], levels_ref, distance, causal
        )
        values = xt_ref[pl.ds(pl.multiple_of(head * HEAD_DIM, HEAD_DIM), HEAD_DIM), :]
        to = pl.ds(pl.multiple_of(at * HEAD_DIM, HEAD_DIM), HEAD_DIM)
        early = low * scores_ref[:half, :half]
        late = jnp.concatenate([far, high], axis=0) * scores_ref[:, half:]
        out_ref[to, :half] = dot(values[:, :half], early)
        out_ref[to, half:] = dot(values, late)
        return carry

    lax.fori_loop(0, heads, one, 0)


def far_coefficients(bits, cum_ref, levels_ref, totals):
    length = cum_ref.shape[1]
    low_bits = length.bit_length() - 1
    last = levels_ref.shape[0] - 1
    decayed = jnp.exp(cum_ref[...])
    before = jnp.zeros(totals[0].shape, F32)
    rows = []
    for bit in range(bits):
        upper = upper_half(bit)
        scale = jnp.where(upper, jnp.exp(before), 0.0)[:, :1]
        rows.append(levels_ref[min(low_bits + 1 + bit, last)] * decayed * scale)
        before = before + jnp.where(upper, totals[bit], 0.0)
    return rows


def mixed_kernel(bits, pieces, *refs):
    came, refs = refs[:bits], refs[bits:]
    intra, refs = refs[:pieces], refs[pieces:]
    (bct_ref, cum_ref, levels_ref, gate_ref, grad_ref, gain_ref,
     mixed_ref, first_ref, second_ref, sums_ref, coef_ref) = refs
    columns, length = mixed_ref.shape
    state = STATE
    rows = far_coefficients(bits, cum_ref, levels_ref, [r[columns:] for r in came])
    for bit in range(bits):
        coef_ref[bit] = rows[bit]
    identity = eye(128)
    c_high, c_low = split(bct_ref[state:])
    square = jnp.zeros((8, length), F32)
    cross = jnp.zeros((8, length), F32)
    step = 128
    each = columns // pieces
    for at in range(0, columns, step):
        part = slice(at, at + step)
        at_head = slice(at // HEAD_DIM, (at + step) // HEAD_DIM)
        ssd = intra[at // each][at % each : at % each + step]
        for bit in range(bits):
            high, low = split(came[bit][part])
            seen = dot_exact(high, c_high) + dot_exact(low, c_high) + dot_exact(high, c_low)
            ssd = ssd + by_head(rows[bit][at_head], seen)
        gate = dot_exact(identity, gate_ref[:, part], (1, 1))
        gate = gate * sigmoid(gate)
        grad = dot_exact(identity, grad_ref[:, part], (1, 1)) * gain_ref[part]
        mixed = ssd * gate
        mixed_ref[part] = mixed
        first_ref[part] = gate * grad
        second_ref[part] = gate * mixed
        square = square + jnp.sum((mixed * mixed).reshape(step // 8, 8, length), axis=0)
        cross = cross + jnp.sum((grad * mixed).reshape(step // 8, 8, length), axis=0)
    sums_ref[0:1] = jnp.sum(square, axis=0, keepdims=True)
    sums_ref[1:2] = jnp.sum(cross, axis=0, keepdims=True)


def level_grad(grad, rows, c_both, c_high, state):
    high, low = split(by_head(rows, grad))
    both = dot_exact(high, c_both)
    return both[:, :state] + both[:, state:] + dot_exact(low, c_high)


def grad_kernel(inner, bits, sums_ref, first_ref, second_ref, bc_ref, coef_ref, grad_ref, level_ref):
    state = STATE
    columns = grad_ref.shape[0]
    inverse = lax.rsqrt(sums_ref[0:1] / inner + EPSILON)
    second = inverse * inverse * inverse * (sums_ref[1:2] / inner)
    c_high, c_low = split(bc_ref[:, state:])
    c_both = jnp.concatenate([c_high, c_low], axis=1)
    step = 128
    for at in range(0, columns, step):
        part = slice(at, at + step)
        at_head = slice(at // HEAD_DIM, (at + step) // HEAD_DIM)
        grad = first_ref[part] * inverse - second_ref[part] * second
        grad_ref[part] = grad
        level_ref[part] = level_grad(grad, coef_ref[bits - 1, at_head], c_both, c_high, state)


def out_kernel(inner, bits, sums_ref, mixed_ref, gain_ref, grad_ref, bc_ref, coef_ref, out_ref, *level_refs):
    state = STATE
    columns = grad_ref.shape[0]
    length = out_ref.shape[0]
    inverse = lax.rsqrt(sums_ref[0:1] / inner + EPSILON)
    c_high, c_low = split(bc_ref[:, state:])
    c_both = jnp.concatenate([c_high, c_low], axis=1)
    identity = eye(length)
    step = 128
    for at in range(0, columns, step):
        part = slice(at, at + step)
        at_head = slice(at // HEAD_DIM, (at + step) // HEAD_DIM)
        grad = grad_ref[part]
        for bit in range(bits - 1):
            level_refs[bit][part] = level_grad(grad, coef_ref[bit, at_head], c_both, c_high, state)
        normed = (gain_ref[part] * mixed_ref[part] * inverse).astype(BF16)
        out_ref[:, part] = dot_exact(identity, normed, (1, 1)).astype(BF16)


def intra_back_kernel(
    first_head, xt_ref, grad_ref, bct_ref, cum_ref, levels_ref, x_out_ref, scores_out_ref,
    scores_ref, cum_t_ref,
):
    heads = x_out_ref.shape[0] // HEAD_DIM
    length = cum_ref.shape[1]
    half = length // 2
    scores_ref[...] = scores_of(bct_ref[...], STATE)
    cum_t_ref[...] = jnp.transpose(cum_ref[...])
    distance, causal = block_masks(half)
    scores_out_ref[...] = jnp.zeros(scores_out_ref.shape, F32)

    def one(at, carry):
        head = first_head + at
        low, far, high = head_weights(
            head, cum_ref, cum_t_ref[...], levels_ref, distance, causal
        )
        where = pl.ds(pl.multiple_of(head * HEAD_DIM, HEAD_DIM), HEAD_DIM)
        values = xt_ref[where, :]
        grads = grad_ref[where, :]
        to = pl.ds(pl.multiple_of(at * HEAD_DIM, HEAD_DIM), HEAD_DIM)
        late = jnp.concatenate([far, high], axis=0)
        back = dot(grads[:, half:], late * scores_ref[:, half:], (1, 1))
        x_out_ref[to, :half] = back[:, :half] + dot(
            grads[:, :half], low * scores_ref[:half, :half], (1, 1)
        )
        x_out_ref[to, half:] = back[:, half:]
        outer = dot(values, grads, (0, 0))
        scores_out_ref[:half, :half] += outer[:half, :half] * low
        scores_out_ref[:, half:] += outer[:, half:] * late
        return carry

    lax.fori_loop(0, heads, one, 0)


def sent_back_kernel(bit, came_ref, level_ref, own_ref, other_ref, *refs):
    *next_refs, sent_ref, share_ref = refs
    heads = own_ref.shape[0] // (HEAD_DIM + 1)
    columns = heads * HEAD_DIM
    upper = upper_half(bit)
    total_grad = came_ref[...]
    if next_refs:
        total_grad = total_grad + next_refs[0][...]
    for_other = jnp.where(upper, jnp.exp(own_ref[columns:]), 1.0)
    for_own = jnp.where(upper, 1.0, jnp.exp(other_ref[columns:]))
    sent_ref[...] = over_heads(for_other, total_grad) + level_ref[...]
    share_ref[...] = over_heads(for_own, total_grad)


def bc_kernel(bits, *refs):
    came, refs = refs[:bits], refs[bits:]
    *score_refs, grad_ref, coef_ref, bct_ref, out_ref = refs
    state = STATE
    columns = grad_ref.shape[0]
    scores = sum(r[...] for r in score_refs)
    out_ref[:state] = dot(bct_ref[state:], scores, (1, 1))
    total = dot(bct_ref[:state], scores)
    identity = eye(state)
    step = 128
    for bit in range(bits):
        for at in range(0, columns, step):
            part = slice(at, at + step)
            at_head = slice(at // HEAD_DIM, (at + step) // HEAD_DIM)
            total = total + dot(
                turn(came[bit][part], identity), by_head(coef_ref[bit, at_head], grad_ref[part])
            )
    out_ref[state:] = total


def last_kernel(pieces, *refs):
    back, refs = refs[:pieces], refs[pieces:]
    (came_ref, share_ref, bct_ref, bct_grad_ref, xt_ref, cum_ref, slope_ref, bc_slope_ref,
     x_out_ref, bc_out_ref) = refs
    state = STATE
    columns, length = xt_ref.shape
    cum = cum_ref[...]
    end_weight = jnp.exp(cum[:, length - 1 :] - cum)
    b_high, b_low = split(bct_ref[:state])
    narrow = eye(state)
    wide = eye(length)
    step = 128
    each = columns // pieces
    b_grad = bct_grad_ref[:state]
    for at in range(0, columns, step):
        part = slice(at, at + step)
        rows = end_weight[at // HEAD_DIM : (at + step) // HEAD_DIM]
        came = came_ref[part] + share_ref[part]
        high, low = split(came)
        seen = dot_exact(high, b_high) + dot_exact(low, b_high) + dot_exact(high, b_low)
        total = back[at // each][at % each : at % each + step] + by_head(rows, seen)
        x_out_ref[:, part] = turn_rows(total, wide) * slope_ref[:, part]
        x_high, x_low = split(by_head(rows, xt_ref[part]))
        t_high = turn_rows_exact(high, narrow)
        t_low = turn_rows_exact(low, narrow)
        b_grad = b_grad + dot_exact(t_high, x_high) + dot_exact(t_high, x_low) + dot_exact(t_low, x_high)
    bc_grad = jnp.concatenate([b_grad, bct_grad_ref[state:]], axis=0)
    bc_out_ref[...] = turn_rows(bc_grad, wide) * bc_slope_ref[...]


def turn_rows(value, identity):
    high, low = split(value)
    return dot_exact(identity, high, (1, 1)) + dot_exact(identity, low, (1, 1))


def turn_rows_exact(value, identity):
    return dot_exact(identity, value, (1, 1)).astype(BF16)


def conv_back_kernel(slope_ref, next_ref, taps_ref, out_ref, rows_ref):
    length = slope_ref.shape[0]
    taps = taps_ref.shape[0]
    rows_ref[:length] = slope_ref[...]
    rows_ref[length:] = next_ref[...]
    out = sum(
        taps_ref[k : k + 1] * rows_ref[taps - 1 - k : taps - 1 - k + length] for k in range(taps)
    )
    out_ref[...] = out.astype(out_ref.dtype)


def shifted(value, axis, steps):
    count = lax.axis_size(axis)
    initial, last = (max(0, -steps), min(count, count - steps))
    return lax.ppermute(value, axis, [(source, source + steps) for source in range(initial, last)])


def partners(count, bit, up=True, down=True):
    route = []
    for low in range(count):
        high = low | 1 << bit
        if high != low and high < count:
            route += [(low, high)] * up + [(high, low)] * down
    return route


def per_device(
    x_raw, bc_raw, gate_raw, log_decay, level_weights, conv_x, conv_bc, norm_gain, out_grad
):
    length, columns = x_raw.shape
    heads = log_decay.shape[0]
    state = STATE
    count = lax.axis_size("ctx")
    bits = count.bit_length() - 1
    inner = HEADS * HEAD_DIM
    gain = norm_gain.reshape(columns, 1)

    tail = jnp.concatenate([x_raw[length - RIM :], bc_raw[length - RIM :]], axis=1)
    rim = shifted(tail, "ctx", 1)
    wide = shape(columns, length)
    xt, slope, bc_conv, bct, bc_slope, cum, own = call(
        pre_kernel,
        [wide, shape(length, columns), shape(length, 2 * state), shape(2 * state, length),
         shape(length, 2 * state), shape(heads, length), shape(columns + heads, state)],
        [x_raw, rim, bc_raw, log_decay, conv_x, conv_bc],
        scratch=[pltpu.VMEM((RIM + length, columns), F32), pltpu.VMEM((RIM + length, 2 * state), F32)],
    )

    pieces = max(bits, 1)
    while heads % pieces or (columns // pieces) % 128:
        pieces += 1
    each = columns // pieces
    intra_scratch = [pltpu.VMEM((length, length), F32), pltpu.VMEM((length, heads), F32)]
    intra = [
        call(
            functools.partial(intra_kernel, piece * heads // pieces),
            [shape(each, length)],
            [xt, bct, cum, level_weights],
            scratch=intra_scratch,
            flops=int(4e9) // pieces,
        )[0]
        for piece in range(pieces)
    ]

    owns, others = [own], []
    for bit in range(bits):
        top = bit == bits - 1
        other = lax.ppermute(owns[-1], "ctx", partners(count, bit, down=not top))
        others.append(other)
        if not top:
            owns += call(
                functools.partial(join_kernel, bit), [shape(columns + heads, state)], [owns[-1], other]
            )

    mixed, first, second, sums, coef = call(
        functools.partial(mixed_kernel, bits, pieces),
        [wide, wide, wide, shape(2, length), shape(bits, heads, length)],
        [*others, *intra, bct, cum, level_weights, gate_raw, out_grad, gain],
    )
    sums = lax.psum(sums, "head")
    grad, top_grad = call(
        functools.partial(grad_kernel, inner, bits),
        [wide, shape(columns, state)],
        [sums, first, second, bc_conv, coef],
    )
    came = lax.ppermute(top_grad, "ctx", partners(count, bits - 1, up=False))
    layer_out, *level_grads = call(
        functools.partial(out_kernel, inner, bits),
        [shape(length, columns, dtype=BF16)] + [shape(columns, state)] * (bits - 1),
        [sums, mixed, gain, grad, bc_conv, coef],
    )
    back = [
        call(
            functools.partial(intra_back_kernel, piece * heads // pieces),
            [shape(each, length), shape(length, length)],
            [xt, grad, bct, cum, level_weights],
            scratch=intra_scratch,
            flops=int(8e9) // pieces,
        )
        for piece in range(pieces)
    ]
    share = []
    for bit in range(bits - 2, -1, -1):
        sent, kept = call(
            functools.partial(sent_back_kernel, bit),
            [shape(columns, state), shape(columns, state)],
            [came, level_grads[bit], owns[bit], others[bit], *share],
        )
        share = [kept]
        came = lax.ppermute(sent, "ctx", partners(count, bit))
    (bct_grad,) = call(
        functools.partial(bc_kernel, bits),
        [shape(2 * state, length)],
        [*others, *[b[1] for b in back], grad, coef, bct],
        flops=int(2e9),
    )
    x_slope, bc_part = call(
        functools.partial(last_kernel, pieces),
        [shape(length, columns), shape(length, 2 * state)],
        [*[b[0] for b in back], came, share[0], bct, bct_grad, xt, cum, slope, bc_slope],
    )
    next_rows = shifted(jnp.concatenate([x_slope[:8], bc_part[:8]], axis=1), "ctx", -1)
    (x_grad,) = call(
        conv_back_kernel,
        [shape(length, columns, dtype=BF16)],
        [x_slope, next_rows[:, :columns], conv_x],
        scratch=[pltpu.VMEM((length + 8, columns), F32)],
    )
    (bc_grad,) = call(
        conv_back_kernel,
        [shape(length, 2 * state)],
        [bc_part, next_rows[:, columns:], conv_bc],
        scratch=[pltpu.VMEM((length + 8, 2 * state), F32)],
    )
    bc_grad = lax.psum(bc_grad, "head").astype(BF16)
    return layer_out, x_grad, bc_grad


def solution(mesh):
    in_specs = (
        P("ctx", "head"),
        P("ctx", None),
        P("ctx", "head"),
        P("head", "ctx"),
        P(None, "head", "ctx"),
        P(None, "head"),
        P(),
        P("head"),
        P("ctx", "head"),
    )
    out_specs = (P("ctx", "head"), P("ctx", "head"), P("ctx", None))
    return jax.shard_map(
        per_device, mesh=mesh, in_specs=in_specs, out_specs=out_specs, check_vma=False
    )
```
